512 devices in a mesh: store: 64 (over y, x, core), mp: 8 (over z).
Axes of the slice: x: 4, y: 8, z: 8, core: 2. Of those that a mesh axis runs over, the one named last changes fastest.
Arguments:
- queries: bfloat16 [32768, 8192], P(('store', 'mp')), may hold values from -6 to 6
- question_keys: bfloat16 [32768, 1024], P(('store', 'mp')), may hold values from -6 to 6
- question_values: bfloat16 [32768, 1024], P(('store', 'mp')), may hold values from -6 to 6
- stored_keys: bfloat16 [512, 128, 1024], P('store', None, 'mp'), may hold values from -6 to 6
- stored_values: bfloat16 [512, 128, 1024], P('store', None, 'mp'), may hold values from -6 to 6
- storage_row: int32 [512], replicated, may hold values from 0 to 511, as said below
- retrieved: int32 [256, 16], P('store'), may hold values from 0 to 511, as said below
Outputs:
- attended: bfloat16 [32768, 8192], P(('store', 'mp'))
The draws below stay inside these ranges and needn't reach their ends.
Inputs may be any that keep to these rules, and one draw needn't show every extreme that they name: storage_row is a permutation; the block at storage row p is held by store index p // 8. `retrieved`: the 4 requests s * 4 to s * 4 + 3 together retrieve 64 blocks held by 64 different store indices, one block from each.
All inputs are finite; a program needn't handle non-finite values.
Results may differ from the reference program's by a relative error of at most 0.009.
Values may be sent and summed in bfloat16 or wider, within the bound.
A program may use at most 64 MiB of HBM per device.

```python
import math
import jax
import jax.numpy as jnp
from jax import lax

QUERY_HEADS = 64
KEY_HEADS = 8
HEAD_SIZE = 128
HEAD_GROUP = 8
REQUEST_TOKENS = 128
BLOCK_TOKENS = 128
CH_DEV = 8
PICKED_BLOCKS = 16
REQUEST_TOTAL = 256
STORED_BLOCKS = 512
QUESTION_TOKENS = 32768


def shared_rows(key):
    return jax.random.permutation(jax.random.fold_in(key, 600), STORED_BLOCKS).astype(jnp.int32)


def draw_queries(key, part):
    key = jax.random.fold_in(key, 11)
    start_offset = jax.random.truncated_normal(key, -6.0, 6.0, (QUESTION_TOKENS, QUERY_HEADS * HEAD_SIZE), jnp.float32)
    return start_offset.astype(jnp.bfloat16)


def draw_stored_keys(key, part):
    key = jax.random.fold_in(key, 12)
    start_offset = jax.random.truncated_normal(key, -6.0, 6.0, (STORED_BLOCKS, BLOCK_TOKENS, KEY_HEADS * HEAD_SIZE), jnp.float32)
    return start_offset.astype(jnp.bfloat16)


def draw_storage_row(key, part):
    storage_rows = shared_rows(key)
    return storage_rows


def lead_with(order, target):
    shift = jnp.argmax(order == target)
    return jnp.roll(order, -shift)


def draw_retrieved(key, part):
    storage_rows = shared_rows(key)
    key = jax.random.fold_in(key, 7)
    inverse = jnp.zeros((STORED_BLOCKS,), jnp.int32).at[storage_rows].set(jnp.arange(STORED_BLOCKS, dtype=jnp.int32))
    store_count = STORED_BLOCKS // CH_DEV
    owner_keys = jax.random.split(key, store_count)
    owners = jax.vmap(lambda item: jax.random.permutation(item, store_count))(owner_keys).astype(jnp.int32)
    first_target = storage_rows[STORED_BLOCKS - 1] // CH_DEV
    second_target = storage_rows[0] // CH_DEV
    owners = owners.at[0].set(lead_with(owners[0], first_target))
    owners = owners.at[1].set(lead_with(owners[1], second_target))
    owners = owners.reshape(REQUEST_TOTAL, PICKED_BLOCKS)
    slot_key = jax.random.fold_in(key, 3)
    local_one = jax.random.randint(slot_key, (REQUEST_TOTAL, PICKED_BLOCKS), 0, CH_DEV)
    local_two = jax.random.randint(jax.random.fold_in(slot_key, 1), (REQUEST_TOTAL, PICKED_BLOCKS), 0, CH_DEV)
    local = jnp.minimum(local_one, local_two).astype(jnp.int32)
    local = local.at[0, 0].set(storage_rows[STORED_BLOCKS - 1] % CH_DEV)
    local = local.at[REQUEST_TOTAL // store_count, 0].set(storage_rows[0] % CH_DEV)
    return inverse[owners * CH_DEV + local].astype(jnp.int32)


def levels(rng, shape, cuts, smallest, top_value):
    def one(dim, shards_of):
        steps = jax.random.uniform(jax.random.fold_in(jax.random.fold_in(rng, 6), dim), (shards_of,), jnp.float32, smallest / len(cuts), top_value / len(cuts))
        return jnp.repeat(jnp.exp(steps), shape[dim] // shards_of).reshape((-1,) + (1,) * (len(shape) - dim - 1))

    loudness = one(*cuts[0])
    for cut in cuts[1:]:
        loudness = loudness * one(*cut)
    return loudness


def centred(key, shape, deviation, bound, shards=(), kind=jnp.bfloat16):
    gain = levels(key, shape, shards, -0.22, 0.18) if shards else 1.0
    values = jax.random.normal(key, shape, jnp.float32) * deviation * gain
    return jnp.minimum(jnp.maximum(values, -bound), bound).astype(kind)


def setup_inputs(seed: int = 0) -> dict:
    splits = jax.random.split(jax.random.key(seed), 8)
    return {
        "queries": draw_queries(jax.random.fold_in(splits[7], 71), 0),
        "question_keys": centred(splits[1], (QUESTION_TOKENS, KEY_HEADS * HEAD_SIZE), 1.0, 6.0, ((0, 512),)),
        "question_values": centred(splits[2], (QUESTION_TOKENS, KEY_HEADS * HEAD_SIZE), 1.0, 6.0, ((0, 512),)),
        "stored_keys": draw_stored_keys(jax.random.fold_in(splits[7], 71), 0),
        "stored_values": centred(splits[4], (STORED_BLOCKS, BLOCK_TOKENS, KEY_HEADS * HEAD_SIZE), 1.0, 6.0, ((0, 64), (2, 8))),
        "storage_row": draw_storage_row(jax.random.fold_in(splits[7], 71), 0),
        "retrieved": draw_retrieved(jax.random.fold_in(splits[7], 71), 0),
    }


def one_request(kernel_inputs, stored_keys, stored_values, storage_row):
    query_slab, key_slab, value_slab, span_ids = kernel_inputs
    scale = 1.0 / math.sqrt(HEAD_SIZE)
    storage_rows = storage_row[span_ids].astype(jnp.int32)
    remote_keys = stored_keys[storage_rows].reshape(PICKED_BLOCKS * BLOCK_TOKENS, KEY_HEADS, HEAD_SIZE).astype(jnp.float32)
    remote_values = stored_values[storage_rows].reshape(PICKED_BLOCKS * BLOCK_TOKENS, KEY_HEADS, HEAD_SIZE).astype(jnp.float32)
    query_head_rows = query_slab.reshape(REQUEST_TOKENS, KEY_HEADS, HEAD_GROUP, HEAD_SIZE).astype(jnp.float32)
    nearby_keys = key_slab.reshape(REQUEST_TOKENS, KEY_HEADS, HEAD_SIZE).astype(jnp.float32)
    nearby_values = value_slab.reshape(REQUEST_TOKENS, KEY_HEADS, HEAD_SIZE).astype(jnp.float32)
    far_scores = jnp.einsum('tgjd,sgd->gjts', query_head_rows, remote_keys) * scale
    near_scores = jnp.einsum('tgjd,sgd->gjts', query_head_rows, nearby_keys) * scale
    causal = jnp.arange(REQUEST_TOKENS)[None, :] <= jnp.arange(REQUEST_TOKENS)[:, None]
    near_scores = jnp.where(causal[None, None], near_scores, -jnp.inf)
    row_max = jnp.maximum(lax.optimization_barrier(jnp.max(far_scores, axis=-1)), lax.optimization_barrier(jnp.max(near_scores, axis=-1)))
    far_weights = jnp.exp(far_scores - row_max[..., None])
    near_weights = jnp.where(causal[None, None], jnp.exp(near_scores - row_max[..., None]), 0.0)
    total = lax.optimization_barrier(jnp.sum(far_weights, axis=-1)) + lax.optimization_barrier(jnp.sum(near_weights, axis=-1))
    far_rounded = far_weights.astype(jnp.bfloat16).astype(jnp.float32)
    near_rounded = near_weights.astype(jnp.bfloat16).astype(jnp.float32)
    summed = jnp.einsum('gjts,sgd->tgjd', far_rounded, remote_values)
    summed = summed + jnp.einsum('gjts,sgd->tgjd', near_rounded, nearby_values)
    result = summed / jnp.transpose(total, (2, 0, 1))[..., None]
    return result.reshape(REQUEST_TOKENS, QUERY_HEADS * HEAD_SIZE).astype(jnp.bfloat16)

def reference(queries, question_keys, question_values, stored_keys, stored_values, storage_row, retrieved):
    kernel_inputs = (queries.reshape(REQUEST_TOTAL, REQUEST_TOKENS, QUERY_HEADS * HEAD_SIZE), question_keys.reshape(REQUEST_TOTAL, REQUEST_TOKENS, KEY_HEADS * HEAD_SIZE), question_values.reshape(REQUEST_TOTAL, REQUEST_TOKENS, KEY_HEADS * HEAD_SIZE), retrieved)
    outputs = lax.map(lambda item: one_request(item, stored_keys, stored_values, storage_row), kernel_inputs)
    return outputs.reshape(QUESTION_TOKENS, QUERY_HEADS * HEAD_SIZE)
```

```python
import functools
import math

import jax
import jax.numpy as jnp
from jax import lax
from jax.experimental import pallas as pl
from jax.experimental.pallas import tpu as pltpu
from jax.sharding import PartitionSpec as P

HEAD = 128
GROUP = 8
TOKENS = 128
CORES = 2
X_CHIPS = 4
HEADS_AT_ONCE = 2
EXPONENT = math.log2(math.e) / math.sqrt(HEAD)
MESH = pl.DeviceIdType.MESH
BF16 = jnp.bfloat16
F32 = jnp.float32


def score_dot(a, b):
    return lax.dot_general(a, b, (((1,), (1,)), ((), ())), preferred_element_type=F32)


def kernel(
    sizes,
    storage_row,
    retrieved,
    queries,
    question_keys,
    question_values,
    stored_keys,
    stored_values,
    out,
    *scratch,
):
    n_y, n_x, n_z, requests, picked = sizes
    ring = n_y // 2
    members = n_x * CORES
    halves = n_z // requests
    part = TOKENS // halves
    width = GROUP * HEAD
    (
        table,
        tables,
        tables_smem,
        stage,
        recv,
        q_all,
        kn_all,
        vn_all,
        o_stage,
        scores,
        local_sem,
        table_send,
        table_recv,
        ring_send,
        ring_recv,
        blk_send,
        blk_recv,
        z_send,
        z_recv,
        o_send,
        o_recv,
    ) = scratch[:21]
    up_keys, up_values, down_keys, down_values = (
        scratch[21 + ring * i : 21 + ring * (i + 1)] for i in range(4)
    )

    store = lax.axis_index("store")
    z = lax.axis_index("mp")
    y = store // members
    member = store % members
    y_up = lax.rem(y + 1, n_y) * members + member
    y_down = lax.rem(y + n_y - 1, n_y) * members + member

    def peer(j):
        return y * members + lax.rem(member + j, members)

    def z_peer(j):
        return lax.rem(z + j, n_z)

    barrier = pltpu.get_barrier_semaphore()
    for target in (y_up, y_down):
        pl.semaphore_signal(barrier, inc=1, device_id=(target, z), device_id_type=MESH)
    for j in range(1, members):
        pl.semaphore_signal(barrier, inc=1, device_id=(peer(j), z), device_id_type=MESH)
    for j in range(1, n_z):
        pl.semaphore_signal(barrier, inc=1, device_id=(store, z_peer(j)), device_id_type=MESH)

    lane = lax.broadcasted_iota(jnp.int32, (8, 128), 1)

    def note(i, value):
        row = storage_row[retrieved[i // picked, lax.rem(i, picked)]]
        return jnp.where(lane == row // 8, lax.rem(row, 8), value)

    table[...] = lax.fori_loop(0, requests * picked, note, jnp.zeros((8, 128), jnp.int32))
    pl.semaphore_wait(barrier, 2 + members - 1 + n_z - 1)

    def remote(src, dst, send, recv_sem, device):
        return pltpu.make_async_remote_copy(
            src_ref=src,
            dst_ref=dst,
            send_sem=send,
            recv_sem=recv_sem,
            device_id=device,
            device_id_type=MESH,
        )

    def table_copy(j):
        return remote(
            table, tables.at[member], table_send.at[j], table_recv.at[j], (peer(j), z)
        )

    for j in range(1, members):
        table_copy(j).start()

    def ring_copy(step, way, kind):
        bufs = ((up_keys, up_values), (down_keys, down_values))[way][kind]
        src = (stored_keys, stored_values)[kind] if step == 1 else bufs[step - 2]
        return remote(
            src,
            bufs[step - 1],
            ring_send.at[step - 1, way, kind],
            ring_recv.at[step - 1, way, kind],
            ((y_up, y_down)[way], z),
        )

    def in_ring(step, way, kind):
        return step < ring or (step == ring and way == kind)

    for kind in range(2):
        for way in range(2):
            if in_ring(1, way, kind):
                ring_copy(1, way, kind).start()

    def z_copies(j):
        to = z_peer(j)
        wide = pl.ds(pl.multiple_of(to * width, width), width)
        narrow = pl.ds(pl.multiple_of(to * HEAD, HEAD), HEAD)
        return [
            remote(src, dst, z_send.at[j, n], z_recv.at[j, n], (store, to))
            for n, (src, dst) in enumerate(
                (
                    (queries.at[:, wide], q_all.at[z]),
                    (question_keys.at[:, narrow], kn_all.at[z]),
                    (question_values.at[:, narrow], vn_all.at[z]),
                )
            )
        ]

    for j in range(1, n_z):
        for copy in z_copies(j):
            copy.start()
    wide = pl.ds(pl.multiple_of(z * width, width), width)
    narrow = pl.ds(pl.multiple_of(z * HEAD, HEAD), HEAD)
    own = [
        pltpu.make_async_copy(queries.at[:, wide], q_all.at[z], local_sem.at[0]),
        pltpu.make_async_copy(question_keys.at[:, narrow], kn_all.at[z], local_sem.at[1]),
        pltpu.make_async_copy(question_values.at[:, narrow], vn_all.at[z], local_sem.at[2]),
    ]
    for copy in own:
        copy.start()

    tables[member] = table[...]
    for j in range(1, members):
        table_copy(j).wait()
    to_smem = pltpu.make_async_copy(tables, tables_smem, local_sem.at[3])
    to_smem.start()
    to_smem.wait()

    def block_copy(slot, holder, j):
        return remote(
            stage.at[slot, j],
            recv.at[holder],
            blk_send.at[slot, j],
            blk_recv.at[slot, j],
            (peer(j), z),
        )

    def hand_out(slot, offset, keys, values):
        holder = lax.rem(y + n_y + offset, n_y) * members + member

        def one(j, carry):
            pick = tables_smem[lax.rem(member + j, members), 0, holder]
            stage[slot, j, 0] = keys[pick]
            stage[slot, j, 1] = values[pick]
            block_copy(slot, holder, j).start()
            return carry

        lax.fori_loop(1, members, one, 0)
        pick = tables_smem[member, 0, holder]
        recv[holder, 0] = keys[pick]
        recv[holder, 1] = values[pick]

    hand_out(0, 0, stored_keys, stored_values)
    for step in range(1, ring + 1):
        for kind in range(2):
            for way in range(2):
                if in_ring(step, way, kind):
                    ring_copy(step, way, kind).wait_recv()
                    if step < ring and in_ring(step + 1, way, kind):
                        ring_copy(step + 1, way, kind).start()
        if step < ring:
            hand_out(2 * step - 1, -step, up_keys[step - 1], up_values[step - 1])
            hand_out(2 * step, step, down_keys[step - 1], down_values[step - 1])
        else:
            hand_out(2 * step - 1, step, up_keys[step - 1], down_values[step - 1])

    for j in range(1, n_z):
        for copy in z_copies(j):
            copy.wait()
    for copy in own:
        copy.wait()
    for step in range(1, ring + 1):
        for kind in range(2):
            for way in range(2):
                if in_ring(step, way, kind):
                    ring_copy(step, way, kind).wait_send()

    def drain(i, carry):
        block_copy(i // (members - 1), 0, 1 + lax.rem(i, members - 1)).wait()
        return carry

    lax.fori_loop(0, n_y * (members - 1), drain, 0)

    rows = HEADS_AT_ONCE * TOKENS
    far = picked * HEAD

    def attend(request):
        holders = [storage_row[retrieved[request, k]] // 8 for k in range(picked)]
        mine = pl.ds(request * halves, halves)

        def chunk(c, carry):
            columns = [
                pl.ds(pl.multiple_of((c * HEADS_AT_ONCE + i) * HEAD, HEAD), HEAD)
                for i in range(HEADS_AT_ONCE)
            ]
            q = jnp.concatenate(
                [q_all[mine, :, cols].reshape(TOKENS, HEAD) for cols in columns], axis=0
            )
            near = score_dot(q, kn_all[mine].reshape(TOKENS, HEAD))
            token = lax.rem(lax.broadcasted_iota(jnp.int32, (rows, TOKENS), 0), TOKENS)
            key = lax.broadcasted_iota(jnp.int32, (rows, TOKENS), 1)
            near = jnp.where(key <= token, near, -jnp.inf)
            scores[:, far : far + HEAD] = near
            top = near
            for k in range(0, picked, 2):
                pair = jnp.concatenate([recv[holders[k], 0], recv[holders[k + 1], 0]], axis=0)
                s = score_dot(q, pair)
                scores[:, k * HEAD : (k + 2) * HEAD] = s
                top = jnp.maximum(top, jnp.maximum(s[:, :HEAD], s[:, HEAD:]))
            top = jnp.max(top, axis=1, keepdims=True)
            w = jnp.exp2((scores[:, far : far + HEAD] - top) * EXPONENT)
            total = w
            summed = jnp.dot(
                w.astype(BF16), vn_all[mine].reshape(TOKENS, HEAD), preferred_element_type=F32
            )
            for k in range(0, picked, 2):
                pair = jnp.concatenate([recv[holders[k], 1], recv[holders[k + 1], 1]], axis=0)
                w = jnp.exp2((scores[:, k * HEAD : (k + 2) * HEAD] - top) * EXPONENT)
                total = total + (w[:, :HEAD] + w[:, HEAD:])
                summed = summed + jnp.dot(w.astype(BF16), pair, preferred_element_type=F32)
            result = (summed / jnp.sum(total, axis=1, keepdims=True)).astype(BF16)
            for i, cols in enumerate(columns):
                o_stage[mine, :, cols] = result[i * TOKENS : (i + 1) * TOKENS].reshape(
                    halves, part, HEAD
                )
            return carry

        lax.fori_loop(0, GROUP // HEADS_AT_ONCE, chunk, 0)

    base = z // halves
    here = lax.rem(z, halves)
    wide = pl.ds(pl.multiple_of(z * width, width), width)

    def out_copy(source, target):
        return remote(
            o_stage.at[target],
            out.at[:, wide],
            o_send.at[target],
            o_recv.at[source],
            (store, target),
        )

    for i in range(1, requests + 1):
        request = lax.rem(base + i, requests)
        attend(request)
        if i < requests:
            for half in range(halves):
                out_copy(z, request * halves + half).start()
        else:
            keep = pltpu.make_async_copy(o_stage.at[z], out.at[:, wide], local_sem.at[4])
            keep.start()
            for j in range(1, halves):
                out_copy(z, base * halves + lax.rem(here + j, halves)).start()
    keep.wait()
    for j in range(1, n_z):
        out_copy(z, z_peer(j)).wait_send()
        out_copy(z_peer(j), z_peer(j)).wait_recv()


def local(queries, question_keys, question_values, stored_keys, stored_values, storage_row, retrieved):
    n_store, n_z = lax.axis_size("store"), lax.axis_size("mp")
    n_x = X_CHIPS
    members = n_x * CORES
    n_y = n_store // members
    requests, picked = retrieved.shape
    ring = n_y // 2
    part = queries.shape[0]
    width = GROUP * HEAD
    held = stored_keys.shape
    dma = pltpu.SemaphoreType.DMA
    scratch = [
        pltpu.VMEM((8, 128), jnp.int32),
        pltpu.VMEM((members, 8, 128), jnp.int32),
        pltpu.SMEM((members, 8, 128), jnp.int32),
        pltpu.VMEM((n_y, members, 2, TOKENS, HEAD), BF16),
        pltpu.VMEM((n_store, 2, TOKENS, HEAD), BF16),
        pltpu.VMEM((n_z, part, width), BF16),
        pltpu.VMEM((n_z, part, HEAD), BF16),
        pltpu.VMEM((n_z, part, HEAD), BF16),
        pltpu.VMEM((n_z, part, width), BF16),
        pltpu.VMEM((HEADS_AT_ONCE * TOKENS, (picked + 1) * HEAD), F32),
        dma((5,)),
        dma((members,)),
        dma((members,)),
        dma((ring, 2, 2)),
        dma((ring, 2, 2)),
        dma((n_y, members)),
        dma((n_y, members)),
        dma((n_z, 3)),
        dma((n_z, 3)),
        dma((n_z,)),
        dma((n_z,)),
    ] + [pltpu.VMEM(held, BF16)] * (4 * ring)
    vmem = pl.BlockSpec(memory_space=pltpu.VMEM)
    smem = pl.BlockSpec(memory_space=pltpu.SMEM)
    anywhere = pl.BlockSpec(memory_space=pl.ANY)
    return pl.pallas_call(
        functools.partial(kernel, (n_y, n_x, n_z, requests, picked)),
        out_shape=jax.ShapeDtypeStruct(queries.shape, BF16),
        in_specs=[smem, smem, anywhere, anywhere, anywhere, vmem, vmem],
        out_specs=anywhere,
        scratch_shapes=scratch,
        name="retrieve_attend",
        compiler_params=pltpu.CompilerParams(
            collective_id=0, has_side_effects=True, vmem_limit_bytes=56 << 20
        ),
    )(storage_row, retrieved, queries, question_keys, question_values, stored_keys, stored_values)


def solution(mesh):
    return jax.shard_map(
        local,
        mesh=mesh,
        in_specs=(
            P(("store", "mp"), None),
            P(("store", "mp"), None),
            P(("store", "mp"), None),
            P("store", None, "mp"),
            P("store", None, "mp"),
            P(),
            P("store", None),
        ),
        out_specs=P(("store", "mp"), None),
        check_vma=False,
    )
```

```python
import functools
import math

import jax
import jax.numpy as jnp
from jax import lax
from jax.experimental import pallas as pl
from jax.experimental.pallas import tpu as pltpu
from jax.sharding import PartitionSpec as P

HEAD = 128
GROUP = 8
TOKENS = 128
CORES = 2
X_CHIPS = 4
HEADS_AT_ONCE = 2
EXPONENT = math.log2(math.e) / math.sqrt(HEAD)
MESH = pl.DeviceIdType.MESH
BF16 = jnp.bfloat16
F32 = jnp.float32


def score_dot(a, b):
    return lax.dot_general(a, b, (((1,), (1,)), ((), ())), preferred_element_type=F32)


def kernel(
    sizes,
    storage_row,
    retrieved,
    queries,
    question_keys,
    question_values,
    stored_keys,
    stored_values,
    out,
    *scratch,
):
    n_y, n_x, n_z, requests, picked = sizes
    ring = n_y // 2
    members = n_x * CORES
    halves = n_z // requests
    part = TOKENS // halves
    width = GROUP * HEAD
    (
        table,
        tables,
        tables_smem,
        holder_of,
        stage,
        recv,
        q_all,
        kn_all,
        vn_all,
        o_stage,
        scores,
        local_sem,
        table_send,
        table_recv,
        ring_send,
        ring_recv,
        blk_send,
        blk_recv,
        z_send,
        z_recv,
        o_send,
        o_recv,
        keep_sem,
    ) = scratch[:23]
    up_keys, up_values, down_keys, down_values = (
        scratch[23 + ring * i : 23 + ring * (i + 1)] for i in range(4)
    )

    store = lax.axis_index("store")
    z = lax.axis_index("mp")
    y = store // members
    member = store % members
    y_up = lax.rem(y + 1, n_y) * members + member
    y_down = lax.rem(y + n_y - 1, n_y) * members + member

    def peer(j):
        return y * members + lax.rem(member + j, members)

    def z_peer(j):
        return lax.rem(z + j, n_z)

    barrier = pltpu.get_barrier_semaphore()
    for target in (y_up, y_down):
        pl.semaphore_signal(barrier, inc=1, device_id=(target, z), device_id_type=MESH)
    for j in range(1, members):
        pl.semaphore_signal(barrier, inc=1, device_id=(peer(j), z), device_id_type=MESH)
    for j in range(1, n_z):
        pl.semaphore_signal(barrier, inc=1, device_id=(store, z_peer(j)), device_id_type=MESH)

    lane = lax.broadcasted_iota(jnp.int32, (1, 128), 1)

    def note(i, value):
        request, k = i // picked, lax.rem(i, picked)
        row = storage_row[retrieved[request, k]]
        holder_of[request, k] = row // 8
        return jnp.where(lane == row // 8, lax.rem(row, 8), value)

    table[...] = lax.fori_loop(0, requests * picked, note, jnp.zeros((1, 128), jnp.int32))
    pl.semaphore_wait(barrier, 2 + members - 1 + n_z - 1)

    def remote(src, dst, send, recv_sem, device):
        return pltpu.make_async_remote_copy(
            src_ref=src,
            dst_ref=dst,
            send_sem=send,
            recv_sem=recv_sem,
            device_id=device,
            device_id_type=MESH,
        )

    def table_copy(j):
        return remote(
            table, tables.at[member], table_send.at[j], table_recv.at[j], (peer(j), z)
        )

    for j in range(1, members):
        table_copy(j).start()

    def ring_copy(step, way, kind):
        bufs = ((up_keys, up_values), (down_keys, down_values))[way][kind]
        src = (stored_keys, stored_values)[kind] if step == 1 else bufs[step - 2]
        return remote(
            src,
            bufs[step - 1],
            ring_send.at[step - 1, way, kind],
            ring_recv.at[step - 1, way, kind],
            ((y_up, y_down)[way], z),
        )

    def in_ring(step, way, kind):
        return step < ring or (step == ring and way == kind)

    for kind in range(2):
        for way in range(2):
            if in_ring(1, way, kind):
                ring_copy(1, way, kind).start()

    def z_copies(j):
        to = z_peer(j)
        wide = pl.ds(pl.multiple_of(to * width, width), width)
        narrow = pl.ds(pl.multiple_of(to * HEAD, HEAD), HEAD)
        return [
            remote(src, dst, z_send.at[j, n], z_recv.at[j, n], (store, to))
            for n, (src, dst) in enumerate(
                (
                    (queries.at[:, wide], q_all.at[z]),
                    (question_keys.at[:, narrow], kn_all.at[z]),
                    (question_values.at[:, narrow], vn_all.at[z]),
                )
            )
        ]

    tables[member] = table[...]
    for j in range(1, members):
        table_copy(j).wait()
    to_smem = pltpu.make_async_copy(tables, tables_smem, local_sem.at[3])
    to_smem.start()
    to_smem.wait()

    chip, core = member // CORES, lax.rem(member, CORES)
    targets = [
        lax.rem(chip + i, n_x) * CORES + (lax.rem(core + c, CORES) if i == 0 else c)
        for i in range(n_x)
        for c in range(CORES)
    ][1:]

    def hand_out(slot, kind, offset, blocks):
        holder = lax.rem(y + n_y + offset, n_y) * members + member
        for target in targets:
            stage[slot, kind, target] = blocks[tables_smem[target, 0, holder]]
            remote(
                stage.at[slot, kind, target],
                recv.at[holder, kind],
                blk_send.at[target],
                blk_recv.at[member],
                (y * members + target, z),
            ).start()
        recv[holder, kind] = blocks[tables_smem[member, 0, holder]]

    def arrived(parcels):
        for parcel in parcels:
            hand_out(*parcel)

    def all_blocks(other):
        return remote(
            stage.at[:, :, other],
            recv.at[pl.ds(0, n_y)],
            blk_send.at[other],
            blk_recv.at[other],
            (y * members + other, z),
        )

    arrived([(0, 0, 0, stored_keys), (0, 1, 0, stored_values)])
    for j in range(1, n_z):
        for copy in z_copies(j):
            copy.start()
    wide = pl.ds(pl.multiple_of(z * width, width), width)
    narrow = pl.ds(pl.multiple_of(z * HEAD, HEAD), HEAD)
    own = [
        pltpu.make_async_copy(queries.at[:, wide], q_all.at[z], local_sem.at[0]),
        pltpu.make_async_copy(question_keys.at[:, narrow], kn_all.at[z], local_sem.at[1]),
        pltpu.make_async_copy(question_values.at[:, narrow], vn_all.at[z], local_sem.at[2]),
    ]
    for copy in own:
        copy.start()

    for step in range(1, ring + 1):
        for kind in range(2):
            parcels = []
            for way in range(2):
                if in_ring(step, way, kind):
                    ring_copy(step, way, kind).wait_recv()
                    if in_ring(step + 1, way, kind):
                        ring_copy(step + 1, way, kind).start()
                    blocks = ((up_keys, up_values), (down_keys, down_values))[way][kind]
                    slot = 2 * step - 1 + (way if step < ring else 0)
                    parcels.append((slot, kind, (-step, step)[way], blocks[step - 1]))
            arrived(parcels)
    for j in range(1, n_z):
        for copy in z_copies(j):
            copy.wait_recv()
    for copy in own:
        copy.wait()

    for other in targets:
        all_blocks(other).wait_recv()

    rows = HEADS_AT_ONCE * TOKENS
    columns = HEADS_AT_ONCE * HEAD
    far = picked * HEAD
    base = z // halves
    here = lax.rem(z, halves)

    def out_copy(c, source, target):
        mine = pl.ds(pl.multiple_of(z * width + c * columns, columns), columns)
        return remote(
            o_stage.at[target, :, pl.ds(pl.multiple_of(c * columns, columns), columns)],
            out.at[:, mine],
            o_send.at[c, target],
            o_recv.at[c, source],
            (store, target),
        )

    def keep_copy(c):
        mine = pl.ds(pl.multiple_of(z * width + c * columns, columns), columns)
        return pltpu.make_async_copy(
            o_stage.at[z, :, pl.ds(pl.multiple_of(c * columns, columns), columns)],
            out.at[:, mine],
            keep_sem.at[c],
        )

    def heads(c):
        return [
            pl.ds(pl.multiple_of(c * columns + i * HEAD, HEAD), HEAD)
            for i in range(HEADS_AT_ONCE)
        ]

    def score(c, request, buf):
        mine = pl.ds(request * halves, halves)
        q = jnp.concatenate(
            [q_all[mine, :, cols].reshape(TOKENS, HEAD) for cols in heads(c)], axis=0
        )
        near = score_dot(q, kn_all[mine].reshape(TOKENS, HEAD))
        token = lax.rem(lax.broadcasted_iota(jnp.int32, (rows, TOKENS), 0), TOKENS)
        key = lax.broadcasted_iota(jnp.int32, (rows, TOKENS), 1)
        near = jnp.where(key <= token, near, -jnp.inf)
        scores[buf, :, far : far + HEAD] = near
        top = near
        for k in range(0, picked, 2):
            pair = [recv[holder_of[request, k + i], 0] for i in range(2)]
            s = score_dot(q, jnp.concatenate(pair, axis=0))
            scores[buf, :, k * HEAD : (k + 2) * HEAD] = s
            top = jnp.maximum(top, jnp.maximum(s[:, :HEAD], s[:, HEAD:]))
        return jnp.max(top, axis=1, keepdims=True)

    def weigh(c, request, buf, top):
        mine = pl.ds(request * halves, halves)
        w = jnp.exp2((scores[buf, :, far : far + HEAD] - top) * EXPONENT)
        total = w
        summed = jnp.dot(
            w.astype(BF16), vn_all[mine].reshape(TOKENS, HEAD), preferred_element_type=F32
        )
        for k in range(0, picked, 2):
            pair = [recv[holder_of[request, k + i], 1] for i in range(2)]
            w = jnp.exp2((scores[buf, :, k * HEAD : (k + 2) * HEAD] - top) * EXPONENT)
            total = total + (w[:, :HEAD] + w[:, HEAD:])
            summed = summed + jnp.dot(
                w.astype(BF16), jnp.concatenate(pair, axis=0), preferred_element_type=F32
            )
        result = (summed * (1.0 / jnp.sum(total, axis=1, keepdims=True))).astype(BF16)
        for i, cols in enumerate(heads(c)):
            o_stage[mine, :, cols] = result[i * TOKENS : (i + 1) * TOKENS].reshape(
                halves, part, HEAD
            )

    def chunk(c, carry):
        order = [lax.rem(base + i, requests) for i in range(1, requests + 1)]
        top = score(c, order[0], 0)
        for i, request in enumerate(order):
            ahead = score(c, order[i + 1], (i + 1) % 2) if i + 1 < requests else None
            weigh(c, request, i % 2, top)
            top = ahead
            if i + 1 < requests:
                for half in range(halves):
                    out_copy(c, z, request * halves + half).start()
            else:
                keep_copy(c).start()
                for j in range(1, halves):
                    out_copy(c, z, base * halves + lax.rem(here + j, halves)).start()
        return carry

    chunks = GROUP // HEADS_AT_ONCE
    lax.fori_loop(0, chunks, chunk, 0)

    for step in range(1, ring + 1):
        for kind in range(2):
            for way in range(2):
                if in_ring(step, way, kind):
                    ring_copy(step, way, kind).wait_send()
    for j in range(1, n_z):
        for copy in z_copies(j):
            copy.wait_send()
    for other in targets:
        all_blocks(other).wait_send()

    def finish(c, carry):
        keep_copy(c).wait()
        for j in range(1, n_z):
            out_copy(c, z, z_peer(j)).wait_send()
            out_copy(c, z_peer(j), z_peer(j)).wait_recv()
        return carry

    lax.fori_loop(0, chunks, finish, 0)


def local(queries, question_keys, question_values, stored_keys, stored_values, storage_row, retrieved):
    n_store, n_z = lax.axis_size("store"), lax.axis_size("mp")
    n_x = X_CHIPS
    members = n_x * CORES
    n_y = n_store // members
    requests, picked = retrieved.shape
    ring = n_y // 2
    part = queries.shape[0]
    width = GROUP * HEAD
    held = stored_keys.shape
    chunks = GROUP // HEADS_AT_ONCE
    dma = pltpu.SemaphoreType.DMA
    scratch = [
        pltpu.VMEM((1, 128), jnp.int32),
        pltpu.VMEM((members, 1, 128), jnp.int32),
        pltpu.SMEM((members, 1, 128), jnp.int32),
        pltpu.SMEM((requests, picked), jnp.int32),
        pltpu.VMEM((n_y, 2, members, TOKENS, HEAD), BF16),
        pltpu.VMEM((n_store, 2, TOKENS, HEAD), BF16),
        pltpu.VMEM((n_z, part, width), BF16),
        pltpu.VMEM((n_z, part, HEAD), BF16),
        pltpu.VMEM((n_z, part, HEAD), BF16),
        pltpu.VMEM((n_z, part, width), BF16),
        pltpu.VMEM((2, HEADS_AT_ONCE * TOKENS, (picked + 1) * HEAD), F32),
        dma((5,)),
        dma((members,)),
        dma((members,)),
        dma((ring, 2, 2)),
        dma((ring, 2, 2)),
        dma((members,)),
        dma((members,)),
        dma((n_z, 3)),
        dma((n_z, 3)),
        dma((chunks, n_z)),
        dma((chunks, n_z)),
        dma((chunks,)),
    ] + [pltpu.VMEM(held, BF16)] * (4 * ring)
    vmem = pl.BlockSpec(memory_space=pltpu.VMEM)
    smem = pl.BlockSpec(memory_space=pltpu.SMEM)
    anywhere = pl.BlockSpec(memory_space=pl.ANY)
    return pl.pallas_call(
        functools.partial(kernel, (n_y, n_x, n_z, requests, picked)),
        out_shape=jax.ShapeDtypeStruct(queries.shape, BF16),
        in_specs=[smem, smem, anywhere, anywhere, anywhere, vmem, vmem],
        out_specs=anywhere,
        scratch_shapes=scratch,
        name="retrieve_attend",
        compiler_params=pltpu.CompilerParams(
            collective_id=0, has_side_effects=True, vmem_limit_bytes=56 << 20
        ),
    )(storage_row, retrieved, queries, question_keys, question_values, stored_keys, stored_values)


def solution(mesh):
    return jax.shard_map(
        local,
        mesh=mesh,
        in_specs=(
            P(("store", "mp"), None),
            P(("store", "mp"), None),
            P(("store", "mp"), None),
            P("store", None, "mp"),
            P("store", None, "mp"),
            P(),
            P("store", None),
        ),
        out_specs=P(("store", "mp"), None),
        check_vma=False,
    )
```

```python
import functools
import math

import jax
import jax.numpy as jnp
from jax import lax
from jax.experimental import pallas as pl
from jax.experimental.pallas import tpu as pltpu
from jax.sharding import PartitionSpec as P

HEAD = 128
GROUP = 8
TOKENS = 128
CORES = 2
X_CHIPS = 4
HEADS_AT_ONCE = 2
EXPONENT = math.log2(math.e) / math.sqrt(HEAD)
MESH = pl.DeviceIdType.MESH
BF16 = jnp.bfloat16
F32 = jnp.float32


def score_dot(a, b):
    return lax.dot_general(a, b, (((1,), (1,)), ((), ())), preferred_element_type=F32)


def kernel(
    sizes,
    storage_row,
    retrieved,
    queries,
    question_keys,
    question_values,
    stored_keys,
    stored_values,
    out,
    *scratch,
):
    n_y, n_x, n_z, requests, picked = sizes
    ring = n_y // 2
    members = n_x * CORES
    halves = n_z // requests
    part = TOKENS // halves
    width = GROUP * HEAD
    (
        table,
        tables,
        tables_smem,
        holder_of,
        stage,
        recv,
        q_all,
        kn_all,
        vn_all,
        o_stage,
        scores,
        local_sem,
        table_send,
        table_recv,
        ring_send,
        ring_recv,
        blk_send,
        blk_recv,
        z_send,
        z_recv,
        o_send,
        o_recv,
        keep_sem,
    ) = scratch[:23]
    up_keys, up_values, down_keys, down_values = (
        scratch[23 + ring * i : 23 + ring * (i + 1)] for i in range(4)
    )

    store = lax.axis_index("store")
    z = lax.axis_index("mp")
    y = store // members
    member = store % members
    y_up = lax.rem(y + 1, n_y) * members + member
    y_down = lax.rem(y + n_y - 1, n_y) * members + member

    def peer(j):
        return y * members + lax.rem(member + j, members)

    def z_peer(j):
        return lax.rem(z + j, n_z)

    barrier = pltpu.get_barrier_semaphore()
    for target in (y_up, y_down):
        pl.semaphore_signal(barrier, inc=1, device_id=(target, z), device_id_type=MESH)
    for j in range(1, members):
        pl.semaphore_signal(barrier, inc=1, device_id=(peer(j), z), device_id_type=MESH)
    for j in range(1, n_z):
        pl.semaphore_signal(barrier, inc=1, device_id=(store, z_peer(j)), device_id_type=MESH)

    lane = lax.broadcasted_iota(jnp.int32, (1, 128), 1)

    def note(i, value):
        request, k = i // picked, lax.rem(i, picked)
        row = storage_row[retrieved[request, k]]
        holder_of[request, k] = row // 8
        return jnp.where(lane == row // 8, lax.rem(row, 8), value)

    table[...] = lax.fori_loop(0, requests * picked, note, jnp.zeros((1, 128), jnp.int32))
    pl.semaphore_wait(barrier, 2 + members - 1 + n_z - 1)

    def remote(src, dst, send, recv_sem, device):
        return pltpu.make_async_remote_copy(
            src_ref=src,
            dst_ref=dst,
            send_sem=send,
            recv_sem=recv_sem,
            device_id=device,
            device_id_type=MESH,
        )

    def table_copy(j):
        return remote(
            table, tables.at[member], table_send.at[j], table_recv.at[j], (peer(j), z)
        )

    for j in range(1, members):
        table_copy(j).start()

    def ring_copy(step, way, kind):
        bufs = ((up_keys, up_values), (down_keys, down_values))[way][kind]
        src = (stored_keys, stored_values)[kind] if step == 1 else bufs[step - 2]
        return remote(
            src,
            bufs[step - 1],
            ring_send.at[step - 1, way, kind],
            ring_recv.at[step - 1, way, kind],
            ((y_up, y_down)[way], z),
        )

    def in_ring(step, way, kind):
        return step < ring or (step == ring and way == kind)

    for kind in range(2):
        for way in range(2):
            if in_ring(1, way, kind):
                ring_copy(1, way, kind).start()

    def z_copies(j):
        to = z_peer(j)
        wide = pl.ds(pl.multiple_of(to * width, width), width)
        narrow = pl.ds(pl.multiple_of(to * HEAD, HEAD), HEAD)
        return [
            remote(src, dst, z_send.at[j, n], z_recv.at[j, n], (store, to))
            for n, (src, dst) in enumerate(
                (
                    (queries.at[:, wide], q_all.at[z]),
                    (question_keys.at[:, narrow], kn_all.at[z]),
                    (question_values.at[:, narrow], vn_all.at[z]),
                )
            )
        ]

    tables[member] = table[...]
    for j in range(1, members):
        table_copy(j).wait()
    to_smem = pltpu.make_async_copy(tables, tables_smem, local_sem.at[3])
    to_smem.start()
    to_smem.wait()

    chip, core = member // CORES, lax.rem(member, CORES)
    targets = [
        lax.rem(chip + i, n_x) * CORES + (lax.rem(core + c, CORES) if i == 0 else c)
        for i in range(n_x)
        for c in range(CORES)
    ][1:]

    def hand_out(slot, kind, offset, blocks):
        holder = lax.rem(y + n_y + offset, n_y) * members + member
        for target in targets:
            stage[slot, kind, target] = blocks[tables_smem[target, 0, holder]]
            remote(
                stage.at[slot, kind, target],
                recv.at[holder, kind],
                blk_send.at[target],
                blk_recv.at[member],
                (y * members + target, z),
            ).start()
        recv[holder, kind] = blocks[tables_smem[member, 0, holder]]

    def arrived(parcels):
        for parcel in parcels:
            hand_out(*parcel)

    def all_blocks(other):
        return remote(
            stage.at[:, :, other],
            recv.at[pl.ds(0, n_y)],
            blk_send.at[other],
            blk_recv.at[other],
            (y * members + other, z),
        )

    arrived([(0, 0, 0, stored_keys), (0, 1, 0, stored_values)])
    for j in range(1, n_z):
        for copy in z_copies(j):
            copy.start()
    wide = pl.ds(pl.multiple_of(z * width, width), width)
    narrow = pl.ds(pl.multiple_of(z * HEAD, HEAD), HEAD)
    own = [
        pltpu.make_async_copy(queries.at[:, wide], q_all.at[z], local_sem.at[0]),
        pltpu.make_async_copy(question_keys.at[:, narrow], kn_all.at[z], local_sem.at[1]),
        pltpu.make_async_copy(question_values.at[:, narrow], vn_all.at[z], local_sem.at[2]),
    ]
    for copy in own:
        copy.start()

    for step in range(1, ring + 1):
        for kind in range(2):
            parcels = []
            for way in range(2):
                if in_ring(step, way, kind):
                    ring_copy(step, way, kind).wait_recv()
                    if in_ring(step + 1, way, kind):
                        ring_copy(step + 1, way, kind).start()
                    blocks = ((up_keys, up_values), (down_keys, down_values))[way][kind]
                    slot = 2 * step - 1 + (way if step < ring else 0)
                    parcels.append((slot, kind, (-step, step)[way], blocks[step - 1]))
            arrived(parcels)
    for j in range(1, n_z):
        for copy in z_copies(j):
            copy.wait_recv()
    for copy in own:
        copy.wait()

    for other in targets:
        all_blocks(other).wait_recv()

    rows = HEADS_AT_ONCE * TOKENS
    columns = HEADS_AT_ONCE * HEAD
    far = picked * HEAD
    base = z // halves
    here = lax.rem(z, halves)

    def out_copy(c, source, target):
        mine = pl.ds(pl.multiple_of(z * width + c * columns, columns), columns)
        return remote(
            o_stage.at[target, :, pl.ds(pl.multiple_of(c * columns, columns), columns)],
            out.at[:, mine],
            o_send.at[c, target],
            o_recv.at[c, source],
            (store, target),
        )

    def keep_copy(c):
        mine = pl.ds(pl.multiple_of(z * width + c * columns, columns), columns)
        return pltpu.make_async_copy(
            o_stage.at[z, :, pl.ds(pl.multiple_of(c * columns, columns), columns)],
            out.at[:, mine],
            keep_sem.at[c],
        )

    def heads(c):
        return [
            pl.ds(pl.multiple_of(c * columns + i * HEAD, HEAD), HEAD)
            for i in range(HEADS_AT_ONCE)
        ]

    def score(c, request, buf):
        mine = pl.ds(request * halves, halves)
        q = jnp.concatenate(
            [q_all[mine, :, cols].reshape(TOKENS, HEAD) for cols in heads(c)], axis=0
        )
        near = score_dot(q, kn_all[mine].reshape(TOKENS, HEAD))
        token = lax.rem(lax.broadcasted_iota(jnp.int32, (rows, TOKENS), 0), TOKENS)
        key = lax.broadcasted_iota(jnp.int32, (rows, TOKENS), 1)
        near = jnp.where(key <= token, near, -jnp.inf)
        scores[buf, :, far : far + HEAD] = near
        top = near
        for k in range(0, picked, 2):
            pair = [recv[holder_of[request, k + i], 0] for i in range(2)]
            s = score_dot(q, jnp.concatenate(pair, axis=0))
            scores[buf, :, k * HEAD : (k + 2) * HEAD] = s
            top = jnp.maximum(top, jnp.maximum(s[:, :HEAD], s[:, HEAD:]))
        return jnp.max(top, axis=1, keepdims=True)

    def weigh(c, request, buf, top):
        mine = pl.ds(request * halves, halves)
        w = jnp.exp2((scores[buf, :, far : far + HEAD] - top) * EXPONENT)
        total = w
        summed = jnp.dot(
            w.astype(BF16), vn_all[mine].reshape(TOKENS, HEAD), preferred_element_type=F32
        )
        for k in range(0, picked, 2):
            pair = [recv[holder_of[request, k + i], 1] for i in range(2)]
            w = jnp.exp2((scores[buf, :, k * HEAD : (k + 2) * HEAD] - top) * EXPONENT)
            total = total + (w[:, :HEAD] + w[:, HEAD:])
            summed = summed + jnp.dot(
                w.astype(BF16), jnp.concatenate(pair, axis=0), preferred_element_type=F32
            )
        result = (summed * (1.0 / jnp.sum(total, axis=1, keepdims=True))).astype(BF16)
        for i, cols in enumerate(heads(c)):
            o_stage[mine, :, cols] = result[i * TOKENS : (i + 1) * TOKENS].reshape(
                halves, part, HEAD
            )

    def chunk(c, carry):
        order = [lax.rem(base + i, requests) for i in range(1, requests + 1)]
        top = score(c, order[0], 0)
        for i, request in enumerate(order):
            ahead = score(c, order[i + 1], (i + 1) % 2) if i + 1 < requests else None
            weigh(c, request, i % 2, top)
            top = ahead
            if i + 1 < requests:
                for half in range(halves):
                    out_copy(c, z, request * halves + half).start()
            else:
                keep_copy(c).start()
                for j in range(1, halves):
                    out_copy(c, z, base * halves + lax.rem(here + j, halves)).start()
        return carry

    chunks = GROUP // HEADS_AT_ONCE
    lax.fori_loop(0, chunks, chunk, 0)

    for step in range(1, ring + 1):
        for kind in range(2):
            for way in range(2):
                if in_ring(step, way, kind):
                    ring_copy(step, way, kind).wait_send()
    for j in range(1, n_z):
        for copy in z_copies(j):
            copy.wait_send()
    for other in targets:
        all_blocks(other).wait_send()

    def finish(c, carry):
        keep_copy(c).wait()
        for j in range(1, n_z):
            out_copy(c, z, z_peer(j)).wait_send()
            out_copy(c, z_peer(j), z_peer(j)).wait_recv()
        return carry

    lax.fori_loop(0, chunks, finish, 0)


def local(queries, question_keys, question_values, stored_keys, stored_values, storage_row, retrieved):
    n_store, n_z = lax.axis_size("store"), lax.axis_size("mp")
    n_x = X_CHIPS
    members = n_x * CORES
    n_y = n_store // members
    requests, picked = retrieved.shape
    ring = n_y // 2
    part = queries.shape[0]
    width = GROUP * HEAD
    held = stored_keys.shape
    chunks = GROUP // HEADS_AT_ONCE
    dma = pltpu.SemaphoreType.DMA
    scratch = [
        pltpu.VMEM((1, 128), jnp.int32),
        pltpu.VMEM((members, 1, 128), jnp.int32),
        pltpu.SMEM((members, 1, 128), jnp.int32),
        pltpu.SMEM((requests, picked), jnp.int32),
        pltpu.VMEM((n_y, 2, members, TOKENS, HEAD), BF16),
        pltpu.VMEM((n_store, 2, TOKENS, HEAD), BF16),
        pltpu.VMEM((n_z, part, width), BF16),
        pltpu.VMEM((n_z, part, HEAD), BF16),
        pltpu.VMEM((n_z, part, HEAD), BF16),
        pltpu.VMEM((n_z, part, width), BF16),
        pltpu.VMEM((2, HEADS_AT_ONCE * TOKENS, (picked + 1) * HEAD), F32),
        dma((5,)),
        dma((members,)),
        dma((members,)),
        dma((ring, 2, 2)),
        dma((ring, 2, 2)),
        dma((members,)),
        dma((members,)),
        dma((n_z, 3)),
        dma((n_z, 3)),
        dma((chunks, n_z)),
        dma((chunks, n_z)),
        dma((chunks,)),
    ] + [pltpu.VMEM(held, BF16)] * (4 * ring)
    vmem = pl.BlockSpec(memory_space=pltpu.VMEM)
    smem = pl.BlockSpec(memory_space=pltpu.SMEM)
    anywhere = pl.BlockSpec(memory_space=pl.ANY)
    return pl.pallas_call(
        functools.partial(kernel, (n_y, n_x, n_z, requests, picked)),
        out_shape=pltpu.VMEM(queries.shape, BF16),
        in_specs=[smem, smem, anywhere, anywhere, anywhere, vmem, vmem],
        out_specs=vmem,
        scratch_shapes=scratch,
        name="retrieve_attend",
        compiler_params=pltpu.CompilerParams(
            collective_id=0, has_side_effects=True, vmem_limit_bytes=56 << 20
        ),
    )(storage_row, retrieved, queries, question_keys, question_values, stored_keys, stored_values)


def solution(mesh):
    return jax.shard_map(
        local,
        mesh=mesh,
        in_specs=(
            P(("store", "mp"), None),
            P(("store", "mp"), None),
            P(("store", "mp"), None),
            P("store", None, "mp"),
            P("store", None, "mp"),
            P(),
            P("store", None),
        ),
        out_specs=P(("store", "mp"), None),
        check_vma=False,
    )
```

```python
import functools
import math

import jax
import jax.numpy as jnp
from jax import lax
from jax.experimental import pallas as pl
from jax.experimental.pallas import tpu as pltpu
from jax.sharding import PartitionSpec as P

HEAD = 128
GROUP = 8
TOKENS = 128
CORES = 2
X_CHIPS = 4
HEADS_AT_ONCE = 2
EXPONENT = math.log2(math.e) / math.sqrt(HEAD)
MESH = pl.DeviceIdType.MESH
BF16 = jnp.bfloat16
F32 = jnp.float32


def score_dot(a, b):
    return lax.dot_general(a, b, (((1,), (1,)), ((), ())), preferred_element_type=F32)


def kernel(
    sizes,
    storage_row,
    retrieved,
    queries,
    question_keys,
    question_values,
    stored_keys,
    stored_values,
    out,
    *scratch,
):
    n_y, n_x, n_z, requests, picked = sizes
    ring = n_y // 2
    members = n_x * CORES
    halves = n_z // requests
    part = TOKENS // halves
    width = GROUP * HEAD
    (
        table,
        tables,
        tables_smem,
        holder_of,
        stage,
        far_keys,
        far_values,
        q_all,
        kn_all,
        vn_all,
        o_stage,
        scores,
        local_sem,
        table_send,
        table_recv,
        ring_send,
        ring_recv,
        blk_send,
        blk_recv,
        z_send,
        z_recv,
        o_send,
        o_recv,
        keep_sem,
    ) = scratch[:24]
    up_keys, up_values, down_keys, down_values = (
        scratch[24 + ring * i : 24 + ring * (i + 1)] for i in range(4)
    )

    store = lax.axis_index("store")
    z = lax.axis_index("mp")
    y = store // members
    member = store % members
    y_up = lax.rem(y + 1, n_y) * members + member
    y_down = lax.rem(y + n_y - 1, n_y) * members + member

    def peer(j):
        return y * members + lax.rem(member + j, members)

    def z_peer(j):
        return lax.rem(z + j, n_z)

    barrier = pltpu.get_barrier_semaphore()
    for target in (y_up, y_down):
        pl.semaphore_signal(barrier, inc=1, device_id=(target, z), device_id_type=MESH)
    for j in range(1, members):
        pl.semaphore_signal(barrier, inc=1, device_id=(peer(j), z), device_id_type=MESH)
    for j in range(1, n_z):
        pl.semaphore_signal(barrier, inc=1, device_id=(store, z_peer(j)), device_id_type=MESH)

    lane = lax.broadcasted_iota(jnp.int32, (1, 128), 1)

    def note(i, value):
        request, k = i // picked, lax.rem(i, picked)
        row = storage_row[retrieved[request, k]]
        holder_of[request, k] = row // 8
        return jnp.where(lane == row // 8, lax.rem(row, 8), value)

    table[...] = lax.fori_loop(0, requests * picked, note, jnp.zeros((1, 128), jnp.int32))
    pl.semaphore_wait(barrier, 2 + members - 1 + n_z - 1)

    def remote(src, dst, send, recv_sem, device):
        return pltpu.make_async_remote_copy(
            src_ref=src,
            dst_ref=dst,
            send_sem=send,
            recv_sem=recv_sem,
            device_id=device,
            device_id_type=MESH,
        )

    def table_copy(j):
        return remote(
            table, tables.at[member], table_send.at[j], table_recv.at[j], (peer(j), z)
        )

    for j in range(1, members):
        table_copy(j).start()

    def ring_copy(step, way, kind):
        bufs = ((up_keys, up_values), (down_keys, down_values))[way][kind]
        src = (stored_keys, stored_values)[kind] if step == 1 else bufs[step - 2]
        return remote(
            src,
            bufs[step - 1],
            ring_send.at[step - 1, way, kind],
            ring_recv.at[step - 1, way, kind],
            ((y_up, y_down)[way], z),
        )

    def in_ring(step, way, kind):
        return step < ring or (step == ring and way == kind)

    for kind in range(2):
        for way in range(2):
            if in_ring(1, way, kind):
                ring_copy(1, way, kind).start()

    def z_copies(j):
        to = z_peer(j)
        wide = pl.ds(pl.multiple_of(to * width, width), width)
        narrow = pl.ds(pl.multiple_of(to * HEAD, HEAD), HEAD)
        return [
            remote(src, dst, z_send.at[j, n], z_recv.at[j, n], (store, to))
            for n, (src, dst) in enumerate(
                (
                    (queries.at[:, wide], q_all.at[z]),
                    (question_keys.at[:, narrow], kn_all.at[z]),
                    (question_values.at[:, narrow], vn_all.at[z]),
                )
            )
        ]

    tables[member] = table[...]
    for j in range(1, members):
        table_copy(j).wait()
    to_smem = pltpu.make_async_copy(tables, tables_smem, local_sem.at[3])
    to_smem.start()
    to_smem.wait()

    chip, core = member // CORES, lax.rem(member, CORES)
    targets = [
        lax.rem(chip + i, n_x) * CORES + (lax.rem(core + c, CORES) if i == 0 else c)
        for i in range(n_x)
        for c in range(CORES)
    ][1:]

    far = (far_keys, far_values)

    def hand_out(slot, kind, offset, blocks):
        holder = lax.rem(y + n_y + offset, n_y) * members + member
        for target in targets:
            stage[slot, kind, target] = blocks[tables_smem[target, 0, holder]]
            remote(
                stage.at[slot, kind, target],
                far[kind].at[holder],
                blk_send.at[kind, target],
                blk_recv.at[kind, member],
                (y * members + target, z),
            ).start()
        far[kind][holder] = blocks[tables_smem[member, 0, holder]]

    def arrived(parcels):
        for parcel in parcels:
            hand_out(*parcel)

    def all_blocks(kind, other):
        return remote(
            stage.at[:, kind, other],
            far[kind].at[pl.ds(0, n_y)],
            blk_send.at[kind, other],
            blk_recv.at[kind, other],
            (y * members + other, z),
        )

    arrived([(0, 0, 0, stored_keys), (0, 1, 0, stored_values)])
    for j in range(1, n_z):
        for copy in z_copies(j):
            copy.start()
    wide = pl.ds(pl.multiple_of(z * width, width), width)
    narrow = pl.ds(pl.multiple_of(z * HEAD, HEAD), HEAD)
    own = [
        pltpu.make_async_copy(queries.at[:, wide], q_all.at[z], local_sem.at[0]),
        pltpu.make_async_copy(question_keys.at[:, narrow], kn_all.at[z], local_sem.at[1]),
        pltpu.make_async_copy(question_values.at[:, narrow], vn_all.at[z], local_sem.at[2]),
    ]
    for copy in own:
        copy.start()

    for step in range(1, ring + 1):
        for kind in range(2):
            parcels = []
            for way in range(2):
                if in_ring(step, way, kind):
                    ring_copy(step, way, kind).wait_recv()
                    if in_ring(step + 1, way, kind):
                        ring_copy(step + 1, way, kind).start()
                    blocks = ((up_keys, up_values), (down_keys, down_values))[way][kind]
                    slot = 2 * step - 1 + (way if step < ring else 0)
                    parcels.append((slot, kind, (-step, step)[way], blocks[step - 1]))
            arrived(parcels)
    for j in range(1, n_z):
        for copy in z_copies(j):
            copy.wait_recv()
    for copy in own:
        copy.wait()

    for other in targets:
        all_blocks(0, other).wait_recv()

    rows = HEADS_AT_ONCE * TOKENS
    columns = HEADS_AT_ONCE * HEAD
    near_at = picked * HEAD
    base = z // halves
    here = lax.rem(z, halves)

    def out_copy(c, source, target):
        mine = pl.ds(pl.multiple_of(z * width + c * columns, columns), columns)
        return remote(
            o_stage.at[target, :, pl.ds(pl.multiple_of(c * columns, columns), columns)],
            out.at[:, mine],
            o_send.at[c, target],
            o_recv.at[c, source],
            (store, target),
        )

    def keep_copy(c):
        mine = pl.ds(pl.multiple_of(z * width + c * columns, columns), columns)
        return pltpu.make_async_copy(
            o_stage.at[z, :, pl.ds(pl.multiple_of(c * columns, columns), columns)],
            out.at[:, mine],
            keep_sem.at[c],
        )

    def heads(c):
        return [
            pl.ds(pl.multiple_of(c * columns + i * HEAD, HEAD), HEAD)
            for i in range(HEADS_AT_ONCE)
        ]

    def score(c, request, buf):
        mine = pl.ds(request * halves, halves)
        q = jnp.concatenate(
            [q_all[mine, :, cols].reshape(TOKENS, HEAD) for cols in heads(c)], axis=0
        )
        near = score_dot(q, kn_all[mine].reshape(TOKENS, HEAD))
        token = lax.rem(lax.broadcasted_iota(jnp.int32, (rows, TOKENS), 0), TOKENS)
        key = lax.broadcasted_iota(jnp.int32, (rows, TOKENS), 1)
        near = jnp.where(key <= token, near, -jnp.inf)
        scores[buf, :, near_at : near_at + HEAD] = near
        top = near
        for k in range(0, picked, 2):
            pair = [far_keys[holder_of[request, k + i]] for i in range(2)]
            s = score_dot(q, jnp.concatenate(pair, axis=0))
            scores[buf, :, k * HEAD : (k + 2) * HEAD] = s
            top = jnp.maximum(top, jnp.maximum(s[:, :HEAD], s[:, HEAD:]))
        return jnp.max(top, axis=1, keepdims=True)

    def weigh(c, request, buf, top):
        mine = pl.ds(request * halves, halves)
        w = jnp.exp2((scores[buf, :, near_at : near_at + HEAD] - top) * EXPONENT)
        total = w
        summed = jnp.dot(
            w.astype(BF16), vn_all[mine].reshape(TOKENS, HEAD), preferred_element_type=F32
        )
        for k in range(0, picked, 2):
            pair = [far_values[holder_of[request, k + i]] for i in range(2)]
            w = jnp.exp2((scores[buf, :, k * HEAD : (k + 2) * HEAD] - top) * EXPONENT)
            total = total + (w[:, :HEAD] + w[:, HEAD:])
            summed = summed + jnp.dot(
                w.astype(BF16), jnp.concatenate(pair, axis=0), preferred_element_type=F32
            )
        result = (summed * (1.0 / jnp.sum(total, axis=1, keepdims=True))).astype(BF16)
        for i, cols in enumerate(heads(c)):
            o_stage[mine, :, cols] = result[i * TOKENS : (i + 1) * TOKENS].reshape(
                halves, part, HEAD
            )

    def chunk(c, top):
        order = [lax.rem(base + i, requests) for i in range(1, requests + 1)]
        for i, request in enumerate(order):
            if i + 1 < requests:
                ahead = score(c, order[i + 1], (i + 1) % 2)
            else:
                ahead = score(jnp.minimum(c + 1, chunks - 1), order[0], 0)
            weigh(c, request, i % 2, top)
            top = ahead
            if i + 1 < requests:
                for half in range(halves):
                    out_copy(c, z, request * halves + half).start()
            else:
                keep_copy(c).start()
                for j in range(1, halves):
                    out_copy(c, z, base * halves + lax.rem(here + j, halves)).start()
        return top

    chunks = GROUP // HEADS_AT_ONCE
    top = score(0, lax.rem(base + 1, requests), 0)
    for other in targets:
        all_blocks(1, other).wait_recv()
    lax.fori_loop(0, chunks, chunk, top)

    for step in range(1, ring + 1):
        for kind in range(2):
            for way in range(2):
                if in_ring(step, way, kind):
                    ring_copy(step, way, kind).wait_send()
    for j in range(1, n_z):
        for copy in z_copies(j):
            copy.wait_send()
    for kind in range(2):
        for other in targets:
            all_blocks(kind, other).wait_send()

    def finish(c, carry):
        keep_copy(c).wait()
        for j in range(1, n_z):
            out_copy(c, z, z_peer(j)).wait_send()
            out_copy(c, z_peer(j), z_peer(j)).wait_recv()
        return carry

    lax.fori_loop(0, chunks, finish, 0)


def local(queries, question_keys, question_values, stored_keys, stored_values, storage_row, retrieved):
    n_store, n_z = lax.axis_size("store"), lax.axis_size("mp")
    n_x = X_CHIPS
    members = n_x * CORES
    n_y = n_store // members
    requests, picked = retrieved.shape
    ring = n_y // 2
    part = queries.shape[0]
    width = GROUP * HEAD
    held = stored_keys.shape
    chunks = GROUP // HEADS_AT_ONCE
    dma = pltpu.SemaphoreType.DMA
    scratch = [
        pltpu.VMEM((1, 128), jnp.int32),
        pltpu.VMEM((members, 1, 128), jnp.int32),
        pltpu.SMEM((members, 1, 128), jnp.int32),
        pltpu.SMEM((requests, picked), jnp.int32),
        pltpu.VMEM((n_y, 2, members, TOKENS, HEAD), BF16),
        pltpu.VMEM((n_store, TOKENS, HEAD), BF16),
        pltpu.VMEM((n_store, TOKENS, HEAD), BF16),
        pltpu.VMEM((n_z, part, width), BF16),
        pltpu.VMEM((n_z, part, HEAD), BF16),
        pltpu.VMEM((n_z, part, HEAD), BF16),
        pltpu.VMEM((n_z, part, width), BF16),
        pltpu.VMEM((2, HEADS_AT_ONCE * TOKENS, (picked + 1) * HEAD), F32),
        dma((5,)),
        dma((members,)),
        dma((members,)),
        dma((ring, 2, 2)),
        dma((ring, 2, 2)),
        dma((2, members)),
        dma((2, members)),
        dma((n_z, 3)),
        dma((n_z, 3)),
        dma((chunks, n_z)),
        dma((chunks, n_z)),
        dma((chunks,)),
    ] + [pltpu.VMEM(held, BF16)] * (4 * ring)
    vmem = pl.BlockSpec(memory_space=pltpu.VMEM)
    smem = pl.BlockSpec(memory_space=pltpu.SMEM)
    anywhere = pl.BlockSpec(memory_space=pl.ANY)
    return pl.pallas_call(
        functools.partial(kernel, (n_y, n_x, n_z, requests, picked)),
        out_shape=pltpu.VMEM(queries.shape, BF16),
        in_specs=[smem, smem, anywhere, anywhere, anywhere, vmem, vmem],
        out_specs=vmem,
        scratch_shapes=scratch,
        name="retrieve_attend",
        compiler_params=pltpu.CompilerParams(
            collective_id=0, has_side_effects=True, vmem_limit_bytes=56 << 20
        ),
    )(storage_row, retrieved, queries, question_keys, question_values, stored_keys, stored_values)


def solution(mesh):
    return jax.shard_map(
        local,
        mesh=mesh,
        in_specs=(
            P(("store", "mp"), None),
            P(("store", "mp"), None),
            P(("store", "mp"), None),
            P("store", None, "mp"),
            P("store", None, "mp"),
            P(),
            P("store", None),
        ),
        out_specs=P(("store", "mp"), None),
        check_vma=False,
    )
```
